32 devices in a mesh: groups: 1, leaf: 32 (over z, y, x, core).
Axes of the slice: x: 2, y: 2, z: 4, core: 2. Of those that a mesh axis runs over, the one named last changes fastest.
Arguments:
- krylov_basis: float32 [8, 64, 131072], P(None, None, ('groups', 'leaf')), may hold values from -6 to 6
- geometry: float32 [7, 131072], P(None, ('groups', 'leaf')), may hold values from -1 to 1
- near_leaf: int32 [512, 9], P(('groups', 'leaf')), may hold values from 0 to 511, as said below
- far_dev: int32 [512, 16], P(('groups', 'leaf')), may hold values from 0 to 31, all different within a row; in each aligned block of 16 rows (0 to 15, 16 to 31, ...) at most 16 rows name the same one
- far_local: int32 [512, 16], P(('groups', 'leaf')), may hold values from 0 to 15
- ubases: bfloat16 [512, 64, 256], P(('groups', 'leaf')), may hold values from -0.375 to 0.375
- vbases: bfloat16 [512, 64, 256], P(('groups', 'leaf')), may hold values from -0.75 to 0.75
- coupling: bfloat16 [512, 64, 1024], P(('groups', 'leaf')), may hold values from -0.1875 to 0.1875
Outputs:
- hessen: float32 [9, 64], P('groups')
- next_vector: float32 [64, 131072], P(None, ('groups', 'leaf'))
The draws below stay inside these ranges and needn't reach their ends.
Inputs may be any that keep to these rules, and one draw needn't show every extreme that they name: `near_leaf`: row i starts with i itself, then max(i - 16, 0) and min(i + 16, 511); every entry lies within 16 of i. `far_dev`: the 16 entries of a row differ; over the rows of one device each device number appears at most 16 times.
All inputs are finite; a program needn't handle non-finite values.
Results may differ from the reference program's by a relative error of at most 0.0041.
Values may be sent and summed in bfloat16 or wider, within the bound.
A program may use at most 128 MiB of HBM per device.

```python
import math
import jax
import jax.numpy as jnp
import numpy as np
from jax import lax

LEAF = 256
RANK = 64
RHS = 64
LEAF_DEV = 16
NEAR = 9
FAR = 16
KRYLOV = 8
LEAVES = 512
NPTS = 131072
MOST = 16
N_LEAF = 32


def draw_near_leaf(key, part):
    key = jax.random.fold_in(key, 11)
    own = jnp.arange(LEAVES, dtype=jnp.int32)[:, None]
    offsets = jax.random.randint(key, (LEAVES, NEAR), -LEAF_DEV, LEAF_DEV + 1, dtype=jnp.int32)
    picked = jnp.clip(own + offsets, 0, LEAVES - 1)
    picked = picked.at[:, 0].set(own[:, 0])
    picked = picked.at[:, 1].set(jnp.maximum(own[:, 0] - LEAF_DEV, 0))
    picked = picked.at[:, 2].set(jnp.minimum(own[:, 0] + LEAF_DEV, LEAVES - 1))
    return picked.astype(jnp.int32)


def plant(drawn, own_key, smallest, top_value):
    longest = drawn.shape.index(max(drawn.shape))
    spots = []
    for shift in (0, 1):
        where = [jax.random.randint(jax.random.fold_in(own_key, axis), (), 0, length) for axis, length in enumerate(drawn.shape)]
        where[longest] = (where[longest] + shift) % drawn.shape[longest]
        spots.append(tuple(where))
    return drawn.at[spots[0]].set(smallest).at[spots[1]].set(top_value)


def levels(rng, extent, shards, low, high):
    level, own = 1.0, jax.random.fold_in(rng, 6)
    for dim, parts in shards:
        draws = jnp.exp(jax.random.uniform(jax.random.fold_in(own, dim), (parts,), jnp.float32, low / len(shards), high / len(shards)))
        level = level * jnp.repeat(draws, extent[dim] // parts).reshape([-1 if axis == dim else 1 for axis in range(len(extent))])
    return level


def deal_out(key, own, number, rows, number_of, top, limit, skew):
    order = jax.random.permutation(key, number_of)
    heavy_load, ordinary = portions_of(number_of, rows * top, limit, skew, True), portions_of(number_of, rows * top, limit, skew, False)
    places = jnp.arange(number_of)

    def named(sizes, offset_by):
        used = int((sizes > 0).sum())
        fixed = max(1, used // 4)
        passed = fixed + (places - fixed + offset_by * (used - fixed)) % max(1, number_of - fixed)
        return jnp.zeros((number_of,), jnp.int32).at[order[jnp.where(places < fixed, places, passed)]].set(jnp.asarray(sizes, jnp.int32))

    sizes = jnp.where(number % 4 == 0, named(heavy_load, number // 4), named(ordinary, number - number // 4 - 1))
    mixed = jax.random.permutation(jax.random.fold_in(own, 3), number_of)
    donor, taker = mixed[0:number_of // 2 * 2:2], mixed[1:number_of // 2 * 2:2]
    slack = jnp.minimum(sizes[donor] - 1, limit - sizes[taker]) // 2
    slack = jnp.where((donor == order[0]) | (taker == order[0]) | (sizes[taker] == 0), 0, jnp.maximum(slack, 0))
    passed = jax.random.randint(jax.random.fold_in(own, 4), (number_of // 2,), 0, 1 << 20) % (slack + 1)
    sizes = sizes.at[donor].add(-passed).at[taker].add(passed)
    labels = jnp.searchsorted(jnp.cumsum(sizes), jnp.arange(rows * top), side="right").astype(jnp.int32)
    table = labels.reshape(top, rows).T
    table = table[jax.random.permutation(jax.random.fold_in(own, 1), rows)]
    offset_by = jax.random.randint(jax.random.fold_in(own, 2), (rows, 1), 0, top)
    return jnp.take_along_axis(table, (jnp.arange(top)[None, :] + offset_by) % top, axis=1)


def portions_of(number_of, total, reach, slope, full):
    loads = [(1 << 20) // math.isqrt(grade ** slope) + 1 for grade in range(1, number_of + 1)]
    largest = reach if full else min(reach, max(-(-total // number_of), total * loads[0] // sum(loads)))
    least = 1 if total - largest >= number_of - 1 else 0
    holding, rest = [largest] + [least] * (number_of - 1), total - largest - least * (number_of - 1)
    while rest > 0:
        candidates = [i for i in range(1, number_of) if holding[i] < largest] or [i for i in range(1, number_of) if holding[i] < reach]
        pool, left = sum([loads[i] for i in candidates]), rest
        for i in candidates:
            addition = min(reach - holding[i], max(1, left * loads[i] // pool), rest)
            holding[i] = holding[i] + addition
            rest = rest - addition
    return np.array(holding)


def gaussian(rng, shape, scale, reach, split=(), kind=jnp.bfloat16):
    loudness = levels(rng, shape, split, -0.22, 0.18) if split else 1.0
    values = jax.random.normal(rng, shape, jnp.float32) * scale * loudness
    return jnp.minimum(jnp.maximum(values, -reach), reach).astype(kind)


def setup_inputs(seed: int = 0, part: int = 0) -> dict:
    seeds = jax.random.split(jax.random.key(seed), 9)
    part_splits = jax.random.split(jax.random.fold_in(seeds[8], part), 9)
    krylov_basis = gaussian(part_splits[0], (KRYLOV, RHS, NPTS), 1.0, 6.0, ((2, 32),), jnp.float32)
    geometry = jnp.clip(jax.random.uniform(part_splits[1], (7, NPTS), jnp.float32, -1.0, 1.0) * levels(part_splits[1], (7, NPTS), ((1, 32),), -0.4, 0.0), -1.0, 1.0)
    near_leaf = draw_near_leaf(jax.random.fold_in(jax.random.fold_in(seeds[8], part), 71), part)
    far_dev_keys = jax.random.split(jax.random.fold_in(part_splits[3], 1), LEAVES // LEAF_DEV)
    far_dev_turns = jax.random.permutation(jax.random.fold_in(part_splits[3], 3), LEAVES // LEAF_DEV)
    far_dev = jax.vmap(lambda own, number: deal_out(jax.random.fold_in(part_splits[3], 2), own, number, LEAF_DEV, N_LEAF, FAR, MOST, 2))(far_dev_keys, far_dev_turns).reshape((LEAVES, FAR))
    far_local = plant(jax.random.randint(part_splits[4], (LEAVES, FAR), 0, LEAF_DEV), jax.random.fold_in(part_splits[4], 1), 0, LEAF_DEV - 1).astype(jnp.int32)
    ubases = gaussian(part_splits[5], (LEAVES, RANK, LEAF), LEAF ** -0.5, 0.375, ((0, 32),))
    vbases = gaussian(part_splits[6], (LEAVES, RANK, LEAF), RANK ** -0.5, 0.75, ((0, 32),))
    coupling = gaussian(part_splits[7], (LEAVES, RANK, FAR * RANK), (FAR * RANK) ** -0.5, 0.1875, ((0, 32),))
    return dict(krylov_basis=krylov_basis, geometry=geometry, near_leaf=near_leaf, far_dev=far_dev, far_local=far_local, ubases=ubases, vbases=vbases, coupling=coupling)


SOFTENING = 0.01
FOUR_PI = 4.0 * math.pi
EPSILON = 1e-06

def pair_kernel(target, source):
    delta_x = target[0][:, None] - source[0][None, :]
    delta_y = target[1][:, None] - source[1][None, :]
    delta_z = target[2][:, None] - source[2][None, :]
    dist_sq = delta_x * delta_x + delta_y * delta_y + delta_z * delta_z + SOFTENING
    numerator = source[3][None, :] * delta_x + source[4][None, :] * delta_y + source[5][None, :] * delta_z
    return source[6][None, :] * numerator / (FOUR_PI * dist_sq * jnp.sqrt(dist_sq))

def reference(krylov_basis, geometry, near_leaf, far_dev, far_local, ubases, vbases, coupling):
    q_last = krylov_basis[KRYLOV - 1]
    density = q_last.astype(jnp.bfloat16)
    sig_leaf = density.reshape(RHS, LEAVES, LEAF).transpose(1, 0, 2)
    geo_leaf = geometry.reshape(7, LEAVES, LEAF).transpose(1, 0, 2)
    multipole = jnp.einsum('irb,ipb->irp', sig_leaf.astype(jnp.float32), ubases.astype(jnp.float32)).astype(jnp.bfloat16)
    far_glob = far_dev * LEAF_DEV + far_local
    coupled = coupling.reshape(LEAVES, RANK, FAR, RANK)

    def one_leaf(index_leaf):
        neighbours = near_leaf[index_leaf]
        blocks = jax.vmap(pair_kernel, in_axes=(None, 0))(geo_leaf[index_leaf], geo_leaf[neighbours])
        blocks = lax.optimization_barrier(blocks.astype(jnp.bfloat16)).astype(jnp.float32)
        near_part = jnp.einsum('jrb,jab->ra', sig_leaf[neighbours].astype(jnp.float32), blocks)
        fetched = multipole[far_glob[index_leaf]].astype(jnp.float32)
        local_exp = jnp.einsum('krq,pkq->rp', fetched, coupled[index_leaf].astype(jnp.float32))
        local_exp = lax.optimization_barrier(local_exp.astype(jnp.bfloat16)).astype(jnp.float32)
        far_part = jnp.einsum('rp,pa->ra', local_exp, vbases[index_leaf].astype(jnp.float32))
        return near_part + far_part
    applied = lax.map(one_leaf, jnp.arange(LEAVES, dtype=jnp.int32))
    imaged = 0.5 * q_last + applied.transpose(1, 0, 2).reshape(RHS, NPTS)
    coeffs = jnp.einsum('krn,rn->kr', krylov_basis, imaged, precision=lax.Precision.HIGHEST) / NPTS
    orthogonal = imaged - jnp.einsum('kr,krn->rn', coeffs, krylov_basis, precision=lax.Precision.HIGHEST)
    norm_rms = jnp.sqrt(lax.optimization_barrier(jnp.mean(orthogonal * orthogonal, axis=1)) + EPSILON)
    hessen = jnp.concatenate([coeffs, norm_rms[None, :]], axis=0)
    return (hessen, orthogonal / norm_rms[:, None])
```

```python
import functools
import math

import jax
import jax.numpy as jnp
import numpy as np
from jax import lax
from jax.experimental import pallas as pl
from jax.experimental.pallas import tpu as pltpu
from jax.sharding import PartitionSpec as P

SOFTENING = 0.01
FOUR_PI = 4.0 * math.pi
EPSILON = 1e-06
MESH = pl.DeviceIdType.MESH
GROUP = 8
FEATURES = 48
F32, BF16 = jnp.float32, jnp.bfloat16


def selections():
    src = np.zeros((32, FEATURES), np.float32)
    tgt = np.zeros((2, FEATURES, 32), np.float32)
    one, f = 24, 0
    for ps, pt in ((0, 0), (0, 1), (1, 0), (1, 1), (0, 2), (2, 0)):
        for c in range(3):
            src[8 * ps + c, f], tgt[0, f, 8 * pt + c] = -2.0, 1.0
            f += 1
            src[8 * ps + 4 + c, f], tgt[1, f, 8 * pt + c] = 1.0, 1.0
            f += 1
    for p in range(3):
        src[8 * p + 3, f], tgt[0, f, one] = 1.0, 1.0
        src[one, f + 1], tgt[0, f + 1, 8 * p + 3] = 1.0, 1.0
        src[8 * p + 7, f + 2], tgt[1, f + 2, one] = 1.0, 1.0
        f += 3
    return src.astype(BF16), tgt.astype(BF16)


def pieces(q):
    a = q.astype(BF16).astype(F32)
    b = (q - a).astype(BF16).astype(F32)
    c = ((q - a) - b).astype(BF16).astype(F32)
    return jnp.concatenate([a, b, c, jnp.ones_like(a)], axis=0)


def dot(a, b, dims=((1,), (0,))):
    return lax.dot_general(a, b, (dims, ((), ())), preferred_element_type=F32)


def kernel(
    n, leaves, npts,
    near_idx, far_idx, q_hbm, src_sel, tgt_sel, krylov_hbm, u_hbm, v_hbm, c_hbm,
    hess_ref, out_ref,
    kry, ub, vb, cp, qh, dens, feats, every, near, imaged, acc, square, red,
    in_sem, halo_send, halo_recv, ag_send, ag_recv, red_send, red_recv,
):
    me = lax.axis_index("leaf")
    bits = n.bit_length() - 1
    lines = n // GROUP
    low, high = lax.rem(me, GROUP), lax.div(me, GROUP)
    krylov_len = kry.shape[0]
    width = dens.shape[3]
    right, left = lax.rem(me + 1, n), lax.rem(me + n - 1, n)

    def group_peer(d):
        return high * GROUP + lax.rem(low + d, GROUP)

    def line_peer(d):
        return lax.rem(high + d, lines) * GROUP + low

    barrier = pltpu.get_barrier_semaphore()
    peers = [group_peer(d) for d in range(1, GROUP)] + [line_peer(d) for d in range(1, lines)] + [left, right]
    for peer in peers:
        pl.semaphore_signal(barrier, inc=1, device_id={"leaf": peer}, device_id_type=MESH)

    last = krylov_len - 1
    copies = [
        pltpu.make_async_copy(krylov_hbm.at[last], kry.at[last], in_sem.at[0]),
        pltpu.make_async_copy(q_hbm, qh.at[1], in_sem.at[1]),
        pltpu.make_async_copy(u_hbm, ub, in_sem.at[2]),
        pltpu.make_async_copy(c_hbm, cp, in_sem.at[3]),
        pltpu.make_async_copy(v_hbm, vb, in_sem.at[4]),
        pltpu.make_async_copy(krylov_hbm.at[pl.ds(0, last)], kry.at[pl.ds(0, last)], in_sem.at[5]),
    ]
    for copy in copies:
        copy.start()
    copies[0].wait()
    for i in range(leaves):
        dens[1, i] = kry[last, :, i * width:(i + 1) * width].astype(BF16)
    copies[1].wait()
    pl.semaphore_wait(barrier, len(peers))
    halos = []
    for t, (ref, peer, slot) in enumerate(((qh, right, 0), (qh, left, 2), (dens, right, 0), (dens, left, 2))):
        halos.append(pltpu.make_async_remote_copy(
            src_ref=ref.at[1], dst_ref=ref.at[slot], send_sem=halo_send.at[t], recv_sem=halo_recv.at[t],
            device_id={"leaf": peer}, device_id_type=MESH))
        halos[-1].start()

    slot = sum(lax.rem(lax.div(me, 1 << b), 2) * (1 << (bits - 1 - b)) for b in range(bits))
    copies[2].wait()

    @pl.loop(0, leaves)
    def _(i):
        m = dot(ub[i], dens[1, i], ((1,), (1,))).astype(BF16)
        half = m.shape[0] // 2
        every[slot, i] = jnp.concatenate([m[:half], m[half:]], axis=1)

    gathers = []
    for step in range(bits):
        bit, size = 1 << (bits - 1 - step), 1 << step
        peer = me + bit * (1 - 2 * lax.rem(lax.div(me, bit), 2))
        held = every.at[pl.ds(lax.div(slot, size) * size, size)]
        gathers.append(pltpu.make_async_remote_copy(
            src_ref=held, dst_ref=held, send_sem=ag_send.at[step], recv_sem=ag_recv.at[step],
            device_id={"leaf": peer}, device_id_type=MESH))
    gathers[0].start()

    def features(side):
        @pl.loop(0, leaves)
        def _(i):
            at = pl.ds(pl.multiple_of(i * width, width), width)
            parts = pieces(qh[side, :, at])
            feats[side * leaves + i] = dot(parts.T.astype(BF16), src_sel[...]).astype(BF16)

    features(1)
    for t in (0, 2, 1, 3):
        halos[t].wait()
    features(0)
    features(2)

    marks = [1 + (leaves - 3) * (step + 1) // bits for step in range(bits - 1)]

    @pl.loop(0, leaves)
    def _(i):
        for step in range(bits - 1):
            @pl.when(i == marks[step])
            def _():
                gathers[step].wait()
                gathers[step + 1].start()

        at = pl.ds(pl.multiple_of(i * width, width), width)
        parts = pieces(qh[1, :, at]).astype(BF16)
        weights = jnp.concatenate([dot(tgt_sel[0], parts), dot(tgt_sel[1], parts)], axis=1).astype(BF16)
        total = jnp.zeros(near.shape[1:], F32)
        for j in range(near_idx.shape[1]):
            leaf = near_idx[i, j]
            both = dot(feats[leaf], weights)
            root = lax.rsqrt(both[:, :width])
            block = (both[:, width:] * (root * root * root)).astype(BF16)
            total += dot(dens[lax.div(leaf, leaves), lax.rem(leaf, leaves)], block)
        near[i] = total

    for copy in copies[3:]:
        copy.wait()
    gathers[-1].wait()

    acc[...] = jnp.zeros_like(acc)

    @pl.loop(0, leaves)
    def _(i):
        at = pl.ds(pl.multiple_of(i * width, width), width)
        rows = []
        for k in range(far_idx.shape[1]):
            where = far_idx[i, k]
            m = every[lax.div(where, leaves), lax.rem(where, leaves)]
            half = m.shape[1] // 2
            rows += [m[:, :half], m[:, half:]]
        local = dot(cp[i], jnp.concatenate(rows, axis=0)).astype(BF16).astype(F32)
        far = dot(local.T.astype(BF16), vb[i])
        value = 0.5 * kry[last, :, at] + (near[i] + far)
        imaged[:, at] = value
        for k in range(krylov_len):
            prod = kry[k, :, at] * value
            acc[k] += sum(prod[:, s:s + 128] for s in range(0, width, 128))

    lane = lax.broadcasted_iota(jnp.int32, square.shape, 1)
    rows_r = imaged.shape[0]

    def to_rows(columns):
        square[...] = jnp.zeros_like(square)
        held = jnp.zeros((rows_r, 128), F32)
        for k, column in enumerate(columns):
            held = jnp.where(lane[:rows_r] == k, column, held)
        square[0:rows_r, :] = held
        return square[...].T[0:8]

    def all_sum(phase, block):
        for level, (count, mine, peer_of) in enumerate(((GROUP, low, group_peer), (lines, high, line_peer))):
            base = 2 * phase + level
            red[base, mine] = block
            sent = []
            for d in range(1, count):
                sent.append(pltpu.make_async_remote_copy(
                    src_ref=red.at[base, mine], dst_ref=red.at[base, mine],
                    send_sem=red_send.at[base, d], recv_sem=red_recv.at[base, d],
                    device_id={"leaf": peer_of(d)}, device_id_type=MESH))
                sent[-1].start()
            for copy in sent:
                copy.wait()
            block = red[base, 0]
            for d in range(1, count):
                block = block + red[base, d]
        return block

    def to_columns(block):
        square[...] = jnp.zeros_like(square)
        square[0:8, :] = block
        return square[...].T[0:rows_r]

    partial = to_rows([jnp.sum(acc[k], axis=1, keepdims=True) for k in range(krylov_len)])
    coeffs = all_sum(0, partial) * (1.0 / npts)
    hess_ref[0:krylov_len, :] = coeffs[0:krylov_len, 0:rows_r]
    lanes = to_columns(coeffs)
    factor = [jnp.sum(jnp.where(lane[:rows_r] == k, lanes, 0.0), axis=1, keepdims=True) for k in range(krylov_len)]
    for k in range(krylov_len):
        acc[k] = jnp.broadcast_to(factor[k], (rows_r, 128))
    near[0, :, 0:128] = jnp.zeros((rows_r, 128), F32)

    @pl.loop(0, leaves * width // 128)
    def _(i):
        at = pl.ds(pl.multiple_of(i * 128, 128), 128)
        value = imaged[:, at]
        shift = acc[0] * kry[0, :, at]
        for k in range(1, krylov_len):
            shift += acc[k] * kry[k, :, at]
        value = value - shift
        imaged[:, at] = value
        near[0, :, 0:128] += value * value

    squares = all_sum(1, to_rows([jnp.sum(near[0, :, 0:128], axis=1, keepdims=True)]))
    norm = jnp.sqrt(squares * (1.0 / npts) + EPSILON)
    hess_ref[krylov_len:krylov_len + 1, :] = norm[0:1, 0:rows_r]
    inverse = jnp.broadcast_to(1.0 / to_columns(norm)[:, 0:1], (rows_r, width))

    @pl.loop(0, leaves)
    def _(i):
        at = pl.ds(pl.multiple_of(i * width, width), width)
        out_ref[:, at] = imaged[:, at] * inverse


def shards(n, krylov_basis, geometry, near_leaf, far_dev, far_local, ubases, vbases, coupling):
    leaves, rank, width = ubases.shape
    krylov_len, columns, points = krylov_basis.shape
    position = lax.axis_index("leaf")
    bits = n.bit_length() - 1
    near_idx = near_leaf - position * leaves + leaves
    reverse = sum(((far_dev >> b) & 1) << (bits - 1 - b) for b in range(bits))
    far_idx = reverse * leaves + far_local
    x, normal, weight = geometry[0:3], geometry[3:6], geometry[6:7]
    moment = weight * normal * (1.0 / FOUR_PI)
    quantities = jnp.concatenate(
        [
            x,
            jnp.sum(x * x, axis=0, keepdims=True) + 0.5 * SOFTENING,
            moment,
            -jnp.sum(moment * x, axis=0, keepdims=True),
        ],
        axis=0,
    )
    src_sel, tgt_sel = selections()
    lines = n // GROUP
    smem, vmem, hbm = (pl.BlockSpec(memory_space=s) for s in (pltpu.SMEM, pltpu.VMEM, pl.ANY))
    return pl.pallas_call(
        functools.partial(kernel, n, leaves, n * points),
        out_shape=(
            jax.ShapeDtypeStruct((krylov_len + 1, columns), F32),
            jax.ShapeDtypeStruct((columns, points), F32),
        ),
        in_specs=[smem, smem, hbm, vmem, vmem, hbm, hbm, hbm, hbm],
        out_specs=(vmem, vmem),
        scratch_shapes=[
            pltpu.VMEM(krylov_basis.shape, F32),
            pltpu.VMEM(ubases.shape, BF16),
            pltpu.VMEM(vbases.shape, BF16),
            pltpu.VMEM(coupling.shape, BF16),
            pltpu.VMEM((3, 8, points), F32),
            pltpu.VMEM((3, leaves, columns, width), BF16),
            pltpu.VMEM((3 * leaves, width, FEATURES), BF16),
            pltpu.VMEM((n, leaves, rank // 2, 2 * columns), BF16),
            pltpu.VMEM((leaves, columns, width), F32),
            pltpu.VMEM((columns, points), F32),
            pltpu.VMEM((krylov_len, columns, 128), F32),
            pltpu.VMEM((128, 128), F32),
            pltpu.VMEM((4, max(GROUP, lines), 8, 128), F32),
            pltpu.SemaphoreType.DMA((6,)),
            pltpu.SemaphoreType.DMA((4,)),
            pltpu.SemaphoreType.DMA((4,)),
            pltpu.SemaphoreType.DMA((bits,)),
            pltpu.SemaphoreType.DMA((bits,)),
            pltpu.SemaphoreType.DMA((4, max(GROUP, lines))),
            pltpu.SemaphoreType.DMA((4, max(GROUP, lines))),
        ],
        compiler_params=pltpu.CompilerParams(
            collective_id=0, has_side_effects=True, vmem_limit_bytes=56 * 1024 * 1024
        ),
    )(near_idx, far_idx, quantities, jnp.asarray(src_sel), jnp.asarray(tgt_sel), krylov_basis, ubases, vbases, coupling)


def solution(mesh):
    in_specs = (
        P(None, None, ("groups", "leaf")),
        P(None, ("groups", "leaf")),
        P(("groups", "leaf"), None),
        P(("groups", "leaf"), None),
        P(("groups", "leaf"), None),
        P(("groups", "leaf"), None, None),
        P(("groups", "leaf"), None, None),
        P(("groups", "leaf"), None, None),
    )
    out_specs = (P("groups", None), P(None, ("groups", "leaf")))
    return jax.shard_map(
        functools.partial(shards, mesh.shape["leaf"]),
        mesh=mesh, in_specs=in_specs, out_specs=out_specs, check_vma=False,
    )
```

```python
import functools
import math

import jax
import jax.numpy as jnp
import numpy as np
from jax import lax
from jax.experimental import pallas as pl
from jax.experimental.pallas import tpu as pltpu
from jax.sharding import PartitionSpec as P

SOFTENING = 0.01
FOUR_PI = 4.0 * math.pi
EPSILON = 1e-06
MESH = pl.DeviceIdType.MESH
GROUP = 8
FEATURES = 48
MARKS = (4, 11)
F32, BF16 = jnp.float32, jnp.bfloat16


def selections():
    src = np.zeros((32, FEATURES), np.float32)
    tgt = np.zeros((2, FEATURES, 32), np.float32)
    one, f = 24, 0
    for ps, pt in ((0, 0), (0, 1), (1, 0), (1, 1), (0, 2), (2, 0)):
        for c in range(3):
            src[8 * ps + c, f], tgt[0, f, 8 * pt + c] = -2.0, 1.0
            f += 1
            src[8 * ps + 4 + c, f], tgt[1, f, 8 * pt + c] = 1.0, 1.0
            f += 1
    for p in range(3):
        src[8 * p + 3, f], tgt[0, f, one] = 1.0, 1.0
        src[one, f + 1], tgt[0, f + 1, 8 * p + 3] = 1.0, 1.0
        src[8 * p + 7, f + 2], tgt[1, f + 2, one] = 1.0, 1.0
        f += 3
    return src.astype(BF16), tgt.astype(BF16)


def pieces(q):
    a = q.astype(BF16).astype(F32)
    b = (q - a).astype(BF16).astype(F32)
    c = ((q - a) - b).astype(BF16).astype(F32)
    return jnp.concatenate([a, b, c, jnp.ones_like(a)], axis=0)


def dot(a, b, dims=((1,), (0,))):
    return lax.dot_general(a, b, (dims, ((), ())), preferred_element_type=F32)


def kernel(
    n, leaves, npts,
    near_ref, far_dev, far_local, slot_of, geo_ref, src_sel, tgt_sel, krylov_hbm, u_hbm, v_hbm, c_hbm,
    hess_ref, out_ref,
    kry, ub, vb, cp, qh, dens, feats, every, applied, grams, acc, square, red_g, red_p,
    in_sem, halo_send, halo_recv, ag_send, ag_recv, red_send, red_recv,
):
    me = lax.axis_index("leaf")
    bits = n.bit_length() - 1
    lines = n // GROUP
    low, high = lax.rem(me, GROUP), lax.div(me, GROUP)
    krylov_len, rows_r = kry.shape[0], kry.shape[1]
    last = krylov_len - 1
    width = dens.shape[3]
    right, left = lax.rem(me + 1, n), lax.rem(me + n - 1, n)
    pairs = [(k, m) for k in range(krylov_len) for m in range(k, krylov_len)]

    def remote(src, dst, peer, send, recv):
        return pltpu.make_async_remote_copy(
            src_ref=src, dst_ref=dst, send_sem=send, recv_sem=recv,
            device_id={"leaf": peer}, device_id_type=MESH)

    def group_peer(d):
        return high * GROUP + lax.rem(low + d, GROUP)

    def line_peer(d):
        return lax.rem(high + d, lines) * GROUP + low

    barrier = pltpu.get_barrier_semaphore()
    peers = [group_peer(d) for d in range(1, GROUP)] + [line_peer(d) for d in range(1, lines)] + [left, right]
    for peer in peers:
        pl.semaphore_signal(barrier, inc=1, device_id={"leaf": peer}, device_id_type=MESH)

    copies = [
        pltpu.make_async_copy(krylov_hbm.at[last], kry.at[last], in_sem.at[0]),
        pltpu.make_async_copy(u_hbm, ub, in_sem.at[1]),
        pltpu.make_async_copy(krylov_hbm.at[pl.ds(0, last)], kry.at[pl.ds(0, last)], in_sem.at[2]),
        pltpu.make_async_copy(c_hbm, cp, in_sem.at[3]),
        pltpu.make_async_copy(v_hbm, vb, in_sem.at[4]),
    ]
    for copy in copies:
        copy.start()

    geo = geo_ref[...]
    x, normal, weight = geo[0:3], geo[3:6], geo[6:7]
    moment = weight * normal * (1.0 / FOUR_PI)
    sq = x * x
    mx = moment * x
    qh[1] = jnp.concatenate(
        [
            x,
            sq[0:1] + sq[1:2] + sq[2:3] + 0.5 * SOFTENING,
            moment,
            -(mx[0:1] + mx[1:2] + mx[2:3]),
        ],
        axis=0,
    )

    copies[0].wait()
    for i in range(leaves):
        dens[1, i] = kry[last, :, i * width:(i + 1) * width].astype(BF16)
    pl.semaphore_wait(barrier, len(peers))
    halos = []
    for t, (ref, peer, slot) in enumerate(((qh, right, 0), (qh, left, 2), (dens, right, 0), (dens, left, 2))):
        halos.append(remote(ref.at[1], ref.at[slot], peer, halo_send.at[t], halo_recv.at[t]))
        halos[-1].start()

    slot = sum(lax.rem(lax.div(me, 1 << b), 2) * (1 << (bits - 1 - b)) for b in range(bits))
    copies[1].wait()

    @pl.loop(0, leaves, unroll=4)
    def _(i):
        m = dot(ub[i], dens[1, i], ((1,), (1,))).astype(BF16)
        half = m.shape[0] // 2
        every[slot, i] = jnp.concatenate([m[:half], m[half:]], axis=1)

    made = []

    def gather(first, count, leaf, peer):
        view = every.at[pl.ds(first, count), pl.ds(leaf[0], leaf[1])]
        made.append(remote(view, view, peer, ag_send.at[len(made)], ag_recv.at[len(made)]))
        return made[-1]

    def digit(b):
        return lax.rem(lax.div(me, 1 << b), 2)

    def across(b):
        return me + (1 << b) * (1 - 2 * digit(b))

    steps = bits - 3
    size = 1 << steps
    core, inner, outer = digit(0), digit(1), digit(2)

    def region(o, i):
        return (core * 4 + i * 2 + o) * size

    whole, front, back = (0, leaves), (0, leaves // 2), (leaves // 2, leaves // 2)
    highs = [
        gather(lax.div(slot, 1 << t) * (1 << t), 1 << t, whole, across(bits - 1 - t)) for t in range(steps)
    ]
    mine = region(outer, inner)
    first = [gather(mine, size, front, across(2)), gather(mine, size, back, across(1))]
    side0 = [gather(mine, size, whole, across(0))]
    second = [
        gather(region(0, inner), 2 * size, front, across(1)),
        gather(region(outer, 0), size, back, across(2)),
        gather(region(outer, 1), size, back, across(2)),
    ]
    side1 = [
        gather(region(1 - outer, inner), size, front, across(0)),
        gather(region(outer, 1 - inner), size, back, across(0)),
    ]
    side2 = [
        gather(region(0, 1 - inner), 2 * size, front, across(0)),
        gather(region(1 - outer, 0), size, back, across(0)),
        gather(region(1 - outer, 1), size, back, across(0)),
    ]

    def start(many):
        for copy in many:
            copy.start()

    def wait(many):
        for copy in many:
            copy.wait()

    highs[0].start()

    def features(side):
        @pl.loop(0, leaves, unroll=4)
        def _(i):
            at = pl.ds(pl.multiple_of(i * width, width), width)
            parts = pieces(qh[side, :, at])
            feats[side * leaves + i] = dot(parts.T.astype(BF16), src_sel[...]).astype(BF16)

    features(1)

    lane = lax.broadcasted_iota(jnp.int32, (rows_r, 128), 1)

    def to_rows(columns):
        held = jnp.zeros((rows_r, 128), F32)
        for k, column in enumerate(columns):
            held = jnp.where(lane == k, column, held)
        square[...] = jnp.zeros_like(square)
        square[0:rows_r, :] = held
        return square[...].T

    copies[2].wait()

    @pl.loop(0, rows_r // 8)
    def _(g):
        here = pl.ds(pl.multiple_of(g * 8, 8), 8)

        def add(c, sums):
            at = pl.ds(pl.multiple_of(c * 128, 128), 128)
            v = [kry[k, here, at] for k in range(krylov_len)]
            return tuple(s + v[k] * v[m] for s, (k, m) in zip(sums, pairs))

        sums = lax.fori_loop(
            0, leaves * width // 128, add, tuple(jnp.zeros((8, 128), F32) for _ in pairs), unroll=2)
        for t in range(len(pairs)):
            grams[t, here, :] = sums[t]

    def exchange(red, phase, level, block):
        count, own, peer_of = ((GROUP, low, group_peer), (lines, high, line_peer))[level]
        base = 2 * phase + level
        red[level, own] = block
        sent = [
            remote(red.at[level, own], red.at[level, own], peer_of(d), red_send.at[base, d], red_recv.at[base, d])
            for d in range(1, count)
        ]
        start(sent)

        def finish():
            wait(sent)
            total = red[level, 0]
            for d in range(1, count):
                total = total + red[level, d]
            return total

        return finish

    gram_rows = red_g.shape[2]
    block = to_rows([jnp.sum(grams[t], axis=1, keepdims=True) for t in range(len(pairs))])
    group_gram = exchange(red_g, 0, 0, block[0:gram_rows])

    for t in range(1, steps):
        highs[t - 1].wait()
        highs[t].start()
    for t in (0, 2, 1, 3):
        halos[t].wait()
    features(0)
    features(2)
    line_gram = exchange(red_g, 0, 1, group_gram())
    highs[-1].wait()
    start(first + side0)
    base_leaf = lax.axis_index("leaf") * leaves - leaves

    @pl.loop(0, leaves)
    def _(i):
        @pl.when(i == MARKS[0])
        def _():
            wait(first)
            start(second + side1)

        @pl.when(i == MARKS[1])
        def _():
            wait(second)
            start(side2)

        at = pl.ds(pl.multiple_of(i * width, width), width)
        parts = pieces(qh[1, :, at]).astype(BF16)
        weights = jnp.concatenate([dot(tgt_sel[0], parts), dot(tgt_sel[1], parts)], axis=1).astype(BF16)
        total = jnp.zeros((rows_r, width), F32)
        for j in range(near_ref.shape[1]):
            leaf = jnp.clip(near_ref[i, j] - base_leaf, 0, 3 * leaves - 1)
            both = dot(feats[leaf], weights)
            root = lax.rsqrt(both[:, :width])
            block = (both[:, width:] * (root * root * root)).astype(BF16)
            total += dot(dens[lax.div(leaf, leaves), lax.rem(leaf, leaves)], block)
        applied[:, at] = total

    wait(copies[3:])
    wait(side0 + side1 + side2)

    acc[...] = jnp.zeros_like(acc)

    @pl.loop(0, leaves, unroll=2)
    def _(i):
        at = pl.ds(pl.multiple_of(i * width, width), width)
        rows = []
        for k in range(far_dev.shape[1]):
            m = every[slot_of[far_dev[i, k]], far_local[i, k]]
            half = m.shape[1] // 2
            rows += [m[:, :half], m[:, half:]]
        local = dot(cp[i], jnp.concatenate(rows, axis=0)).astype(BF16).astype(F32)
        value = applied[:, at] + dot(local.T.astype(BF16), vb[i])
        applied[:, at] = value
        for k in range(krylov_len + 1):
            prod = value * (kry[k, :, at] if k < krylov_len else value)
            acc[k] += sum(prod[:, s:s + 128] for s in range(0, width, 128))

    part_rows = red_p.shape[2]
    block = to_rows([jnp.sum(acc[k], axis=1, keepdims=True) for k in range(krylov_len + 1)])
    group_part = exchange(red_p, 1, 0, block[0:part_rows])
    gram = line_gram()
    line_part = exchange(red_p, 1, 1, group_part())
    part = line_part()
    scale = 1.0 / npts
    inner_of = {}
    for t, (k, m) in enumerate(pairs):
        inner_of[k, m] = inner_of[m, k] = gram[t:t + 1] * scale
    with_a = [part[k:k + 1] * scale for k in range(krylov_len)]
    coeffs = [with_a[k] + 0.5 * inner_of[k, last] for k in range(krylov_len)]
    shifts = coeffs[:last] + [with_a[last] + 0.5 * (inner_of[last, last] - 1.0)]
    mean = part[krylov_len:krylov_len + 1] * scale
    for k in range(krylov_len):
        along = sum(shifts[m] * inner_of[k, m] for m in range(krylov_len))
        mean = mean + shifts[k] * (along - 2.0 * with_a[k])
    norm = jnp.sqrt(jnp.maximum(mean, 0.0) + EPSILON)
    square[...] = jnp.zeros_like(square)
    for k in range(krylov_len):
        square[k:k + 1, :] = shifts[k]
        square[16 + k:17 + k, :] = coeffs[k]
    hess_ref[0:krylov_len, :] = square[16:16 + krylov_len, 0:rows_r]
    hess_ref[krylov_len:krylov_len + 1, :] = norm[:, 0:rows_r]
    square[krylov_len:krylov_len + 1, :] = 1.0 / norm
    lanes = square[...].T[0:rows_r]
    inverse = jnp.broadcast_to(lanes[:, krylov_len:krylov_len + 1], (rows_r, 128))
    for k in range(krylov_len):
        acc[k] = jnp.broadcast_to(lanes[:, k:k + 1], (rows_r, 128)) * inverse
    acc[krylov_len] = inverse

    @pl.loop(0, leaves * width // 128)
    def _(i):
        at = pl.ds(pl.multiple_of(i * 128, 128), 128)
        value = applied[:, at] * acc[krylov_len]
        for k in range(krylov_len):
            value = value - acc[k] * kry[k, :, at]
        out_ref[:, at] = value


def shards(n, krylov_basis, geometry, near_leaf, far_dev, far_local, ubases, vbases, coupling):
    leaves, rank, width = ubases.shape
    krylov_len, columns, points = krylov_basis.shape
    bits = n.bit_length() - 1
    slot_of = np.array([int(format(d, f"0{bits}b")[::-1], 2) for d in range(n)], np.int32)
    src_sel, tgt_sel = selections()
    lines = n // GROUP
    pairs = krylov_len * (krylov_len + 1) // 2
    smem, vmem, hbm = (pl.BlockSpec(memory_space=s) for s in (pltpu.SMEM, pltpu.VMEM, pl.ANY))
    return pl.pallas_call(
        functools.partial(kernel, n, leaves, n * points),
        out_shape=(
            jax.ShapeDtypeStruct((krylov_len + 1, columns), F32),
            jax.ShapeDtypeStruct((columns, points), F32),
        ),
        in_specs=[smem, smem, smem, smem, vmem, vmem, vmem, hbm, hbm, hbm, hbm],
        out_specs=(vmem, vmem),
        scratch_shapes=[
            pltpu.VMEM(krylov_basis.shape, F32),
            pltpu.VMEM(ubases.shape, BF16),
            pltpu.VMEM(vbases.shape, BF16),
            pltpu.VMEM(coupling.shape, BF16),
            pltpu.VMEM((3, 8, points), F32),
            pltpu.VMEM((3, leaves, columns, width), BF16),
            pltpu.VMEM((3 * leaves, width, FEATURES), BF16),
            pltpu.VMEM((n, leaves, rank // 2, 2 * columns), BF16),
            pltpu.VMEM((columns, points), F32),
            pltpu.VMEM((pairs, columns, 128), F32),
            pltpu.VMEM((krylov_len + 1, columns, 128), F32),
            pltpu.VMEM((128, 128), F32),
            pltpu.VMEM((2, max(GROUP, lines), -(-pairs // 8) * 8, 128), F32),
            pltpu.VMEM((2, max(GROUP, lines), 16, 128), F32),
            pltpu.SemaphoreType.DMA((5,)),
            pltpu.SemaphoreType.DMA((4,)),
            pltpu.SemaphoreType.DMA((4,)),
            pltpu.SemaphoreType.DMA((bits + 8,)),
            pltpu.SemaphoreType.DMA((bits + 8,)),
            pltpu.SemaphoreType.DMA((4, max(GROUP, lines))),
            pltpu.SemaphoreType.DMA((4, max(GROUP, lines))),
        ],
        compiler_params=pltpu.CompilerParams(
            collective_id=0, has_side_effects=True, vmem_limit_bytes=56 * 1024 * 1024
        ),
    )(
        near_leaf, far_dev, far_local, jnp.asarray(slot_of), geometry, jnp.asarray(src_sel), jnp.asarray(tgt_sel),
        krylov_basis, ubases, vbases, coupling,
    )


def solution(mesh):
    in_specs = (
        P(None, None, ("groups", "leaf")),
        P(None, ("groups", "leaf")),
        P(("groups", "leaf"), None),
        P(("groups", "leaf"), None),
        P(("groups", "leaf"), None),
        P(("groups", "leaf"), None, None),
        P(("groups", "leaf"), None, None),
        P(("groups", "leaf"), None, None),
    )
    out_specs = (P("groups", None), P(None, ("groups", "leaf")))
    return jax.shard_map(
        functools.partial(shards, mesh.shape["leaf"]),
        mesh=mesh, in_specs=in_specs, out_specs=out_specs, check_vma=False,
    )
```

```python
import functools
import math

import jax
import jax.numpy as jnp
import numpy as np
from jax import lax
from jax.experimental import pallas as pl
from jax.experimental.pallas import tpu as pltpu
from jax.sharding import PartitionSpec as P

SOFTENING = 0.01
FOUR_PI = 4.0 * math.pi
EPSILON = 1e-06
MESH = pl.DeviceIdType.MESH
GROUP = 8
FEATURES = 48
MARKS = (4, 11)
F32, BF16 = jnp.float32, jnp.bfloat16


def selections():
    src = np.zeros((32, FEATURES), np.float32)
    tgt = np.zeros((2, FEATURES, 32), np.float32)
    one, f = 24, 0
    for ps, pt in ((0, 0), (0, 1), (1, 0), (1, 1), (0, 2), (2, 0)):
        for c in range(3):
            src[8 * ps + c, f], tgt[0, f, 8 * pt + c] = -2.0, 1.0
            f += 1
            src[8 * ps + 4 + c, f], tgt[1, f, 8 * pt + c] = 1.0, 1.0
            f += 1
    for p in range(3):
        src[8 * p + 3, f], tgt[0, f, one] = 1.0, 1.0
        src[one, f + 1], tgt[0, f + 1, 8 * p + 3] = 1.0, 1.0
        src[8 * p + 7, f + 2], tgt[1, f + 2, one] = 1.0, 1.0
        f += 3
    return src.astype(BF16), tgt.astype(BF16)


def pieces(q):
    a = q.astype(BF16).astype(F32)
    b = (q - a).astype(BF16).astype(F32)
    c = ((q - a) - b).astype(BF16).astype(F32)
    return jnp.concatenate([a, b, c, jnp.ones_like(a)], axis=0)


def dot(a, b, dims=((1,), (0,))):
    return lax.dot_general(a, b, (dims, ((), ())), preferred_element_type=F32)


def kernel(
    n, leaves, npts,
    near_ref, far_dev, far_local, slot_of, geo_ref, src_sel, tgt_sel, krylov_hbm, u_hbm, v_hbm, c_hbm,
    hess_ref, out_ref,
    kry, ub, vb, cp, qh, dens, feats, every, applied, grams, acc, square, red_g, red_p,
    in_sem, halo_send, halo_recv, ag_send, ag_recv, red_send, red_recv,
):
    me = lax.axis_index("leaf")
    bits = n.bit_length() - 1
    lines = n // GROUP
    low, high = lax.rem(me, GROUP), lax.div(me, GROUP)
    krylov_len, rows_r = kry.shape[0], kry.shape[1]
    last = krylov_len - 1
    width = dens.shape[3]
    right, left = lax.rem(me + 1, n), lax.rem(me + n - 1, n)
    pairs = [(k, m) for k in range(krylov_len) for m in range(k, krylov_len)]

    def remote(src, dst, peer, send, recv):
        return pltpu.make_async_remote_copy(
            src_ref=src, dst_ref=dst, send_sem=send, recv_sem=recv,
            device_id={"leaf": peer}, device_id_type=MESH)

    def group_peer(d):
        return high * GROUP + lax.rem(low + d, GROUP)

    def line_peer(d):
        return lax.rem(high + d, lines) * GROUP + low

    barrier = pltpu.get_barrier_semaphore()
    peers = [group_peer(d) for d in range(1, GROUP)] + [line_peer(d) for d in range(1, lines)] + [left, right]
    for peer in peers:
        pl.semaphore_signal(barrier, inc=1, device_id={"leaf": peer}, device_id_type=MESH)

    copies = [
        pltpu.make_async_copy(krylov_hbm.at[last], kry.at[last], in_sem.at[0]),
        pltpu.make_async_copy(u_hbm, ub, in_sem.at[1]),
        pltpu.make_async_copy(krylov_hbm.at[pl.ds(0, last)], kry.at[pl.ds(0, last)], in_sem.at[2]),
        pltpu.make_async_copy(c_hbm, cp, in_sem.at[3]),
        pltpu.make_async_copy(v_hbm, vb, in_sem.at[4]),
    ]
    copies[0].start()

    geo = geo_ref[...]
    x, normal, weight = geo[0:3], geo[3:6], geo[6:7]
    moment = weight * normal * (1.0 / FOUR_PI)
    sq = x * x
    mx = moment * x
    qh[1] = jnp.concatenate(
        [
            x,
            sq[0:1] + sq[1:2] + sq[2:3] + 0.5 * SOFTENING,
            moment,
            -(mx[0:1] + mx[1:2] + mx[2:3]),
        ],
        axis=0,
    )

    copies[0].wait()
    for copy in copies[1:]:
        copy.start()
    for i in range(leaves):
        dens[1, i] = kry[last, :, i * width:(i + 1) * width].astype(BF16)
    pl.semaphore_wait(barrier, len(peers))
    halos = []
    for t, (ref, peer, slot) in enumerate(((qh, right, 0), (qh, left, 2), (dens, right, 0), (dens, left, 2))):
        halos.append(remote(ref.at[1], ref.at[slot], peer, halo_send.at[t], halo_recv.at[t]))
        halos[-1].start()

    slot = sum(lax.rem(lax.div(me, 1 << b), 2) * (1 << (bits - 1 - b)) for b in range(bits))
    copies[1].wait()

    @pl.loop(0, leaves, unroll=4)
    def _(i):
        m = dot(ub[i], dens[1, i], ((1,), (1,))).astype(BF16)
        half = m.shape[0] // 2
        every[slot, i] = jnp.concatenate([m[:half], m[half:]], axis=1)

    made = []

    def gather(first, count, leaf, peer):
        view = every.at[pl.ds(first, count), pl.ds(leaf[0], leaf[1])]
        made.append(remote(view, view, peer, ag_send.at[len(made)], ag_recv.at[len(made)]))
        return made[-1]

    def digit(b):
        return lax.rem(lax.div(me, 1 << b), 2)

    def across(b):
        return me + (1 << b) * (1 - 2 * digit(b))

    steps = bits - 3
    size = 1 << steps
    core, inner, outer = digit(0), digit(1), digit(2)

    def region(o, i):
        return (core * 4 + i * 2 + o) * size

    whole, front, back = (0, leaves), (0, leaves // 2), (leaves // 2, leaves // 2)
    highs = [
        gather(lax.div(slot, 1 << t) * (1 << t), 1 << t, whole, across(bits - 1 - t)) for t in range(steps)
    ]
    mine = region(outer, inner)
    first = [gather(mine, size, front, across(2)), gather(mine, size, back, across(1))]
    side0 = [gather(mine, size, whole, across(0))]
    second = [
        gather(region(0, inner), 2 * size, front, across(1)),
        gather(region(outer, 0), size, back, across(2)),
        gather(region(outer, 1), size, back, across(2)),
    ]
    side1 = [
        gather(region(1 - outer, inner), size, front, across(0)),
        gather(region(outer, 1 - inner), size, back, across(0)),
    ]
    side2 = [
        gather(region(0, 1 - inner), 2 * size, front, across(0)),
        gather(region(1 - outer, 0), size, back, across(0)),
        gather(region(1 - outer, 1), size, back, across(0)),
    ]

    def start(many):
        for copy in many:
            copy.start()

    def wait(many):
        for copy in many:
            copy.wait()

    highs[0].start()

    def features(side):
        @pl.loop(0, leaves, unroll=4)
        def _(i):
            at = pl.ds(pl.multiple_of(i * width, width), width)
            parts = pieces(qh[side, :, at])
            feats[side * leaves + i] = dot(parts.T.astype(BF16), src_sel[...]).astype(BF16)

    features(1)

    lane = lax.broadcasted_iota(jnp.int32, (rows_r, 128), 1)

    def to_rows(columns):
        held = jnp.zeros((rows_r, 128), F32)
        for k, column in enumerate(columns):
            held = jnp.where(lane == k, column, held)
        square[...] = jnp.zeros_like(square)
        square[0:rows_r, :] = held
        return square[...].T

    copies[2].wait()

    @pl.loop(0, rows_r // 8)
    def _(g):
        here = pl.ds(pl.multiple_of(g * 8, 8), 8)

        def add(c, sums):
            at = pl.ds(pl.multiple_of(c * 128, 128), 128)
            v = [kry[k, here, at] for k in range(krylov_len)]
            return tuple(s + v[k] * v[m] for s, (k, m) in zip(sums, pairs))

        sums = lax.fori_loop(
            0, leaves * width // 128, add, tuple(jnp.zeros((8, 128), F32) for _ in pairs), unroll=2)
        for t in range(len(pairs)):
            grams[t, here, :] = sums[t]

    def exchange(red, phase, level, block):
        count, own, peer_of = ((GROUP, low, group_peer), (lines, high, line_peer))[level]
        base = 2 * phase + level
        red[level, own] = block
        sent = [
            remote(red.at[level, own], red.at[level, own], peer_of(d), red_send.at[base, d], red_recv.at[base, d])
            for d in range(1, count)
        ]
        start(sent)

        def finish():
            wait(sent)
            total = red[level, 0]
            for d in range(1, count):
                total = total + red[level, d]
            return total

        return finish

    gram_rows = red_g.shape[2]
    block = to_rows([jnp.sum(grams[t], axis=1, keepdims=True) for t in range(len(pairs))])
    group_gram = exchange(red_g, 0, 0, block[0:gram_rows])

    for t in range(1, steps):
        highs[t - 1].wait()
        highs[t].start()
    for t in (0, 2, 1, 3):
        halos[t].wait()
    features(0)
    features(2)
    line_gram = exchange(red_g, 0, 1, group_gram())
    highs[-1].wait()
    start(first + side0)
    base_leaf = lax.axis_index("leaf") * leaves - leaves

    @pl.loop(0, leaves)
    def _(i):
        @pl.when(i == MARKS[0])
        def _():
            wait(first)
            start(second + side1)

        @pl.when(i == MARKS[1])
        def _():
            wait(second)
            start(side2)

        at = pl.ds(pl.multiple_of(i * width, width), width)
        parts = pieces(qh[1, :, at]).astype(BF16)
        weights = jnp.concatenate([dot(tgt_sel[0], parts), dot(tgt_sel[1], parts)], axis=1).astype(BF16)
        total = jnp.zeros((rows_r, width), F32)
        for j in range(near_ref.shape[1]):
            leaf = jnp.clip(near_ref[i, j] - base_leaf, 0, 3 * leaves - 1)
            both = dot(feats[leaf], weights)
            root = lax.rsqrt(both[:, :width])
            block = (both[:, width:] * (root * root * root)).astype(BF16)
            total += dot(dens[lax.div(leaf, leaves), lax.rem(leaf, leaves)], block)
        applied[:, at] = total

    wait(copies[3:])
    wait(side0 + side1 + side2)

    acc[...] = jnp.zeros_like(acc)

    @pl.loop(0, leaves, unroll=2)
    def _(i):
        at = pl.ds(pl.multiple_of(i * width, width), width)
        rows = []
        for k in range(far_dev.shape[1]):
            m = every[slot_of[far_dev[i, k]], far_local[i, k]]
            half = m.shape[1] // 2
            rows += [m[:, :half], m[:, half:]]
        local = dot(cp[i], jnp.concatenate(rows, axis=0)).astype(BF16).astype(F32)
        value = applied[:, at] + dot(local.T.astype(BF16), vb[i])
        applied[:, at] = value
        for k in range(krylov_len + 1):
            prod = value * (kry[k, :, at] if k < krylov_len else value)
            acc[k] += sum(prod[:, s:s + 128] for s in range(0, width, 128))

    part_rows = red_p.shape[2]
    block = to_rows([jnp.sum(acc[k], axis=1, keepdims=True) for k in range(krylov_len + 1)])
    group_part = exchange(red_p, 1, 0, block[0:part_rows])
    gram = line_gram()
    line_part = exchange(red_p, 1, 1, group_part())
    part = line_part()
    scale = 1.0 / npts
    inner_of = {}
    for t, (k, m) in enumerate(pairs):
        inner_of[k, m] = inner_of[m, k] = gram[t:t + 1] * scale
    with_a = [part[k:k + 1] * scale for k in range(krylov_len)]
    coeffs = [with_a[k] + 0.5 * inner_of[k, last] for k in range(krylov_len)]
    shifts = coeffs[:last] + [with_a[last] + 0.5 * (inner_of[last, last] - 1.0)]
    mean = part[krylov_len:krylov_len + 1] * scale
    for k in range(krylov_len):
        along = sum(shifts[m] * inner_of[k, m] for m in range(krylov_len))
        mean = mean + shifts[k] * (along - 2.0 * with_a[k])
    norm = jnp.sqrt(jnp.maximum(mean, 0.0) + EPSILON)
    square[...] = jnp.zeros_like(square)
    for k in range(krylov_len):
        square[k:k + 1, :] = shifts[k]
        square[16 + k:17 + k, :] = coeffs[k]
    hess_ref[0:krylov_len, :] = square[16:16 + krylov_len, 0:rows_r]
    hess_ref[krylov_len:krylov_len + 1, :] = norm[:, 0:rows_r]
    square[krylov_len:krylov_len + 1, :] = 1.0 / norm
    lanes = square[...].T[0:rows_r]
    inverse = jnp.broadcast_to(lanes[:, krylov_len:krylov_len + 1], (rows_r, 128))
    for k in range(krylov_len):
        acc[k] = jnp.broadcast_to(lanes[:, k:k + 1], (rows_r, 128)) * inverse
    acc[krylov_len] = inverse

    @pl.loop(0, leaves * width // 128)
    def _(i):
        at = pl.ds(pl.multiple_of(i * 128, 128), 128)
        value = applied[:, at] * acc[krylov_len]
        for k in range(krylov_len):
            value = value - acc[k] * kry[k, :, at]
        out_ref[:, at] = value


def shards(n, krylov_basis, geometry, near_leaf, far_dev, far_local, ubases, vbases, coupling):
    leaves, rank, width = ubases.shape
    krylov_len, columns, points = krylov_basis.shape
    bits = n.bit_length() - 1
    slot_of = np.array([int(format(d, f"0{bits}b")[::-1], 2) for d in range(n)], np.int32)
    src_sel, tgt_sel = selections()
    lines = n // GROUP
    pairs = krylov_len * (krylov_len + 1) // 2
    smem, vmem, hbm = (pl.BlockSpec(memory_space=s) for s in (pltpu.SMEM, pltpu.VMEM, pl.ANY))
    return pl.pallas_call(
        functools.partial(kernel, n, leaves, n * points),
        out_shape=(
            jax.ShapeDtypeStruct((krylov_len + 1, columns), F32),
            jax.ShapeDtypeStruct((columns, points), F32),
        ),
        in_specs=[smem, smem, smem, smem, vmem, vmem, vmem, hbm, hbm, hbm, hbm],
        out_specs=(vmem, vmem),
        scratch_shapes=[
            pltpu.VMEM(krylov_basis.shape, F32),
            pltpu.VMEM(ubases.shape, BF16),
            pltpu.VMEM(vbases.shape, BF16),
            pltpu.VMEM(coupling.shape, BF16),
            pltpu.VMEM((3, 8, points), F32),
            pltpu.VMEM((3, leaves, columns, width), BF16),
            pltpu.VMEM((3 * leaves, width, FEATURES), BF16),
            pltpu.VMEM((n, leaves, rank // 2, 2 * columns), BF16),
            pltpu.VMEM((columns, points), F32),
            pltpu.VMEM((pairs, columns, 128), F32),
            pltpu.VMEM((krylov_len + 1, columns, 128), F32),
            pltpu.VMEM((128, 128), F32),
            pltpu.VMEM((2, max(GROUP, lines), -(-pairs // 8) * 8, 128), F32),
            pltpu.VMEM((2, max(GROUP, lines), 16, 128), F32),
            pltpu.SemaphoreType.DMA((5,)),
            pltpu.SemaphoreType.DMA((4,)),
            pltpu.SemaphoreType.DMA((4,)),
            pltpu.SemaphoreType.DMA((bits + 8,)),
            pltpu.SemaphoreType.DMA((bits + 8,)),
            pltpu.SemaphoreType.DMA((4, max(GROUP, lines))),
            pltpu.SemaphoreType.DMA((4, max(GROUP, lines))),
        ],
        compiler_params=pltpu.CompilerParams(
            collective_id=0, has_side_effects=True, vmem_limit_bytes=56 * 1024 * 1024
        ),
    )(
        near_leaf, far_dev, far_local, jnp.asarray(slot_of), geometry, jnp.asarray(src_sel), jnp.asarray(tgt_sel),
        krylov_basis, ubases, vbases, coupling,
    )


def solution(mesh):
    in_specs = (
        P(None, None, ("groups", "leaf")),
        P(None, ("groups", "leaf")),
        P(("groups", "leaf"), None),
        P(("groups", "leaf"), None),
        P(("groups", "leaf"), None),
        P(("groups", "leaf"), None, None),
        P(("groups", "leaf"), None, None),
        P(("groups", "leaf"), None, None),
    )
    out_specs = (P("groups", None), P(None, ("groups", "leaf")))
    return jax.shard_map(
        functools.partial(shards, mesh.shape["leaf"]),
        mesh=mesh, in_specs=in_specs, out_specs=out_specs, check_vma=False,
    )
```
